32 devices in a mesh: pair: 2 (over x), vblk: 16 (over z, y, core).
Axes of the slice: x: 2, y: 2, z: 4, core: 2. Of those that a mesh axis runs over, the one named last changes fastest.
Arguments:
- factors: bfloat16 [1536, 80, 512], P('pair', 'vblk'), may hold values from -2.5 to 2.5
- amplitudes: bfloat16 [8, 512, 512], P(None, ('pair', 'vblk')), may hold values from -0.01171875 to 0.01171875
Outputs:
- ladder: float32 [8, 80, 2, 5], P('pair', 'vblk')
The draws below stay inside these ranges and needn't reach their ends.
All inputs are finite; a program needn't handle non-finite values.
Results may differ from the reference program's by a relative error of at most 0.0003.
Values may be sent and summed in bfloat16 or wider, within the bound.
A program may use at most 64 MiB of HBM per device.

```python
import jax
import jax.numpy as jnp
from jax import lax

V = 512
Q = 1536
P_SIZE = 8
A_DEV = 5
STEPS = 2
BLOCKS = 16
AWIN = 80


def block_levels(stream_key, extent, pieces, least, largest):
    def one(position, blocks):
        steps = jax.random.uniform(jax.random.fold_in(jax.random.fold_in(stream_key, 6), position), (blocks,), jnp.float32, least / len(pieces), largest / len(pieces))
        return jnp.repeat(jnp.exp(steps), extent[position] // blocks).reshape((-1,) + (1,) * (len(extent) - position - 1))

    factor_of = one(*pieces[0])
    for cut in pieces[1:]:
        factor_of = factor_of * one(*cut)
    return factor_of


def normal_values(key, shape, deviation, reach, pieces=(), dtype=jnp.bfloat16):
    drawn = jax.random.normal(key, shape, jnp.float32) * deviation
    if len(pieces) > 0:
        drawn = block_levels(key, shape, pieces, -0.22, 0.18) * drawn
    return jnp.clip(drawn, min=-reach, max=reach).astype(dtype)


def setup_inputs(seed: int = 0) -> dict:
    splits = jax.random.split(jax.random.key(seed), 3)
    return {
        "factors": normal_values(splits[0], (Q, AWIN, V), 0.16, 2.5, ((0, 2), (1, 16))),
        "amplitudes": normal_values(splits[1], (P_SIZE, V, V), (V * V) ** -0.5, 0.01171875, ((1, 32),)),
    }


def reference(factors, amplitudes):
    factor_f = factors.astype(jnp.float32)
    amplitude_f = amplitudes.astype(jnp.float32)
    blocks = factor_f.reshape(Q, BLOCKS, A_DEV, V)
    rolled = [jnp.roll(blocks, step_index, axis=1) for step_index in range(STEPS)]
    partner = jnp.stack(rolled, axis=2).reshape(Q, BLOCKS, STEPS * A_DEV, V)

    def block_ladder(inputs):
        own_block, partner_block = inputs
        integrals = jnp.einsum("qac,qbd->acbd", own_block, partner_block, precision=lax.Precision.HIGHEST)
        return jnp.einsum("pcd,acbd->pab", amplitude_f, integrals, precision=lax.Precision.HIGHEST)

    per_block = lax.map(block_ladder, (blocks.transpose(1, 0, 2, 3), partner.transpose(1, 0, 2, 3)))
    return per_block.transpose(1, 0, 2, 3).reshape(P_SIZE, AWIN, STEPS, A_DEV)
```

```python
import functools
import math

import jax
import jax.numpy as jnp
from jax import lax
from jax.experimental import pallas as pl
from jax.experimental.pallas import tpu as pltpu
from jax.sharding import PartitionSpec as P

STEPS = 2
MESH = pl.DeviceIdType.MESH
F32 = jnp.float32
BF16 = jnp.bfloat16


def shifted(value, axis, steps):
    count = lax.axis_size(axis)
    pairs = [(source, (source + steps) % count) for source in range(count)]
    return lax.ppermute(value, axis, pairs)


def general_body(factors, amplitudes):
    aux_rows = factors.shape[0]
    block_rows = factors.shape[1]
    pair_count = amplitudes.shape[0]
    virtuals = amplitudes.shape[2]
    partner = jnp.concatenate([factors, shifted(factors, "vblk", 1)], axis=1)
    running = jnp.zeros((pair_count, block_rows, STEPS * block_rows), F32)
    amp_piece = lax.all_gather(amplitudes, ("pair", "vblk"), axis=1, tiled=True)
    row_count = amp_piece.shape[1]
    group_size = math.gcd(row_count, 64)
    block_count = row_count // group_size
    piece_blocks = amp_piece.reshape(pair_count, block_count, group_size, virtuals).transpose(
        1, 0, 2, 3
    )
    own_parts = factors.reshape(aux_rows, block_rows, block_count, group_size).transpose(2, 0, 1, 3)

    def one_block(carried, pieces):
        piece_part, own_part = pieces
        integrals = jnp.einsum("qac,qbd->acbd", own_part, partner, preferred_element_type=F32)
        update = jnp.einsum(
            "pcd,acbd->pab", piece_part.astype(F32), integrals, precision=lax.Precision.HIGHEST
        )
        return (carried + update, None)

    running, unused = lax.scan(one_block, running, (piece_blocks, own_parts))
    partial_ladder = running.reshape(pair_count, block_rows, STEPS, block_rows)
    return lax.psum_scatter(partial_ladder, "pair", scatter_dimension=0, tiled=True)


def kernel(dims, fac, amp, out, nb, fact, tall, wst, acc, red, part, recv, send, fsend, frecv, xs, xr):
    nx, nz, ny, nk = dims
    nv = nz * ny * nk
    blocks, aux, virt = fac.shape
    pairs, rows, _ = amp.shape
    group = 2 * rows
    groups = virt // group
    wide = 2 * pairs * rows

    x = lax.axis_index("pair")
    v = lax.axis_index("vblk")
    z, y, k = v // (ny * nk), (v // nk) % ny, v % nk

    def place(zz, yy, kk):
        return (zz * ny + yy) * nk + kk

    zs = [lax.rem(z + i, nz) for i in range(nz)]
    nxt, prv = lax.rem(v + 1, nv), lax.rem(v + nv - 1, nv)
    to_y, to_k = (x, place(z, 1 - y, k)), (x, place(z, y, 1 - k))
    to_x = (1 - x, v)

    barrier = pltpu.get_barrier_semaphore()
    peers = [(x, place(zz, y, k)) for zz in zs[1:]] + [to_y, to_k, to_x, (x, nxt), (x, prv)]
    for peer in peers:
        pl.semaphore_signal(barrier, inc=1, device_id=peer, device_id_type=MESH)
    pl.semaphore_wait(barrier, len(peers))

    sends = []

    def push(src, piece, target):
        copy = pltpu.make_async_remote_copy(
            src_ref=src,
            dst_ref=tall.at[piece],
            send_sem=send.at[len(sends)],
            recv_sem=recv.at[piece],
            device_id=target,
            device_id_type=MESH,
        )
        copy.start()
        sends.append(copy)

    def arrived(piece):
        pltpu.make_async_remote_copy(
            src_ref=amp,
            dst_ref=tall.at[piece],
            send_sem=send.at[0],
            recv_sem=recv.at[piece],
            device_id=to_x,
            device_id_type=MESH,
        ).wait_recv()

    def factor(j):
        return pltpu.make_async_remote_copy(
            src_ref=fac.at[j],
            dst_ref=nb.at[j],
            send_sem=fsend.at[j],
            recv_sem=frecv.at[j],
            device_id=(x, nxt),
            device_id_type=MESH,
        )

    mine = x * nv + v
    for zz in zs[1:]:
        push(amp, mine, (x, place(zz, y, k)))
    push(amp, mine, to_y)
    push(amp, mine, to_x)
    push(amp, mine, to_k)
    for j in range(blocks):
        factor(j).start()
    tall[pl.ds(mine, 1)] = amp[...][None]

    def stage_z():
        for zz in zs[1:]:
            piece = x * nv + place(zz, y, k)
            arrived(piece)
            for target in (to_y, to_x, to_k):
                push(tall.at[piece], piece, target)

    def stage_y():
        for zz in zs:
            piece = x * nv + place(zz, 1 - y, k)
            arrived(piece)
            for target in (to_x, to_k):
                push(tall.at[piece], piece, target)

    def stage_x(ys):
        for yy in ys:
            for zz in zs:
                piece = (1 - x) * nv + place(zz, yy, k)
                arrived(piece)
                push(tall.at[piece], piece, to_k)

    def stage_k():
        for xx in (x, 1 - x):
            for yy in (y, 1 - y):
                for zz in zs:
                    arrived(xx * nv + place(zz, yy, 1 - k))

    half = virt // 2

    def integrals(src, j):
        def one(i, _):
            a = i // 2
            start = pl.multiple_of(lax.rem(i, 2) * half, half)
            w = jnp.dot(
                fact[a, pl.ds(start, half), :], src[j], preferred_element_type=F32
            )
            high = w.astype(BF16)
            wst[j, 0, a, pl.ds(start, half), :] = high
            wst[j, 1, a, pl.ds(start, half), :] = (w - high.astype(F32)).astype(BF16)
            return 0

        lax.fori_loop(0, 2 * blocks, one, 0)

    def contract(s, j):
        acc[...] = jnp.zeros_like(acc)

        def one(g, _):
            lhs = wst[j, :, :, pl.ds(pl.multiple_of(g * group, group), group), :]
            lhs = lhs.reshape(2 * blocks * group, virt)
            rhs = tall[pl.ds(2 * g, 2)].reshape(wide, virt)
            acc[...] += lax.dot_general(
                lhs, rhs, (((1,), (1,)), ((), ())), preferred_element_type=F32
            )
            return 0

        lax.fori_loop(0, groups, one, 0)
        full = acc[...].reshape(2, blocks, group, wide)
        full = full[0] + full[1]
        row = lax.broadcasted_iota(jnp.int32, (blocks, group, wide), 1)
        col = lax.broadcasted_iota(jnp.int32, (blocks, group, wide), 2)
        own = (col // (pairs * rows)) * rows + col % rows
        red[s * blocks + j] = jnp.sum(jnp.where(row == own, full, 0.0), axis=1)

    def turn(a, _):
        fact[a] = fac[a].T
        return 0

    lax.fori_loop(0, blocks, turn, 0)
    integrals(fac, 0)
    integrals(fac, 1)
    stage_z()
    integrals(fac, 2)
    integrals(fac, 3)
    stage_y()
    integrals(fac, 4)
    stage_x([y])
    stage_x([1 - y])
    stage_k()
    for j in range(blocks):
        contract(0, j)
    for j in range(blocks):
        factor(j).wait_recv()
        integrals(nb, j)
        contract(1, j)

    swap = pltpu.make_async_remote_copy(
        src_ref=red, dst_ref=part, send_sem=xs, recv_sem=xr, device_id=to_x, device_id_type=MESH
    )
    swap.start()
    for copy in sends:
        copy.wait_send()
    for j in range(blocks):
        factor(j).wait_send()
    swap.wait()
    out[...] = red[...] + part[...]


def staged_body(dims, factors, amplitudes):
    aux, blocks, virt = factors.shape
    pairs, rows, _ = amplitudes.shape
    pieces = dims[0] * dims[1] * dims[2] * dims[3]
    wide = 2 * pairs * rows
    nsends = 3 * (dims[1] - 1) + (dims[1] + 2) + 2 * dims[1] + 2 * dims[1]
    vmem = pl.BlockSpec(memory_space=pltpu.VMEM)
    sums = pl.pallas_call(
        functools.partial(kernel, dims),
        out_shape=jax.ShapeDtypeStruct((STEPS * blocks, blocks, wide), F32),
        in_specs=[vmem, vmem],
        out_specs=vmem,
        scratch_shapes=[
            pltpu.VMEM((blocks, aux, virt), BF16),
            pltpu.VMEM((blocks, virt, aux), BF16),
            pltpu.VMEM((pieces, pairs, rows, virt), BF16),
            pltpu.VMEM((blocks, 2, blocks, virt, virt), BF16),
            pltpu.VMEM((2 * blocks * 2 * rows, wide), F32),
            pltpu.VMEM((STEPS * blocks, blocks, wide), F32),
            pltpu.VMEM((STEPS * blocks, blocks, wide), F32),
            pltpu.SemaphoreType.DMA((pieces,)),
            pltpu.SemaphoreType.DMA((pieces,)),
            pltpu.SemaphoreType.DMA((blocks,)),
            pltpu.SemaphoreType.DMA((blocks,)),
            pltpu.SemaphoreType.DMA,
            pltpu.SemaphoreType.DMA,
        ],
        compiler_params=pltpu.CompilerParams(
            collective_id=0, has_side_effects=True, vmem_limit_bytes=56 * 1024 * 1024
        ),
    )(factors.transpose(1, 0, 2), amplitudes)
    share = pairs // dims[0]
    sums = sums.reshape(STEPS, blocks, blocks, 2, pairs, rows).sum(axis=(3, 5))
    sums = sums.transpose(3, 2, 0, 1)
    return lax.dynamic_slice_in_dim(sums, lax.axis_index("pair") * share, share, 0)


def solution(mesh):
    placed = (P("pair", "vblk", None), P(None, ("pair", "vblk"), None))
    staged = mesh.shape["pair"] == 2 and mesh.shape["vblk"] == 16
    body = functools.partial(staged_body, (2, 4, 2, 2)) if staged else general_body
    return jax.shard_map(
        body, mesh=mesh, in_specs=placed, out_specs=P("pair", "vblk", None, None), check_vma=False
    )
```

```python
import functools
import math

import jax
import jax.numpy as jnp
from jax import lax
from jax.experimental import pallas as pl
from jax.experimental.pallas import tpu as pltpu
from jax.sharding import PartitionSpec as P

STEPS = 2
MESH = pl.DeviceIdType.MESH
F32 = jnp.float32
BF16 = jnp.bfloat16


def shifted(value, axis, steps):
    count = lax.axis_size(axis)
    pairs = [(source, (source + steps) % count) for source in range(count)]
    return lax.ppermute(value, axis, pairs)


def general_body(factors, amplitudes):
    aux_rows = factors.shape[0]
    block_rows = factors.shape[1]
    pair_count = amplitudes.shape[0]
    virtuals = amplitudes.shape[2]
    partner = jnp.concatenate([factors, shifted(factors, "vblk", 1)], axis=1)
    running = jnp.zeros((pair_count, block_rows, STEPS * block_rows), F32)
    amp_piece = lax.all_gather(amplitudes, ("pair", "vblk"), axis=1, tiled=True)
    row_count = amp_piece.shape[1]
    group_size = math.gcd(row_count, 64)
    block_count = row_count // group_size
    piece_blocks = amp_piece.reshape(pair_count, block_count, group_size, virtuals).transpose(
        1, 0, 2, 3
    )
    own_parts = factors.reshape(aux_rows, block_rows, block_count, group_size).transpose(2, 0, 1, 3)

    def one_block(carried, pieces):
        piece_part, own_part = pieces
        integrals = jnp.einsum("qac,qbd->acbd", own_part, partner, preferred_element_type=F32)
        update = jnp.einsum(
            "pcd,acbd->pab", piece_part.astype(F32), integrals, precision=lax.Precision.HIGHEST
        )
        return (carried + update, None)

    running, unused = lax.scan(one_block, running, (piece_blocks, own_parts))
    partial_ladder = running.reshape(pair_count, block_rows, STEPS, block_rows)
    return lax.psum_scatter(partial_ladder, "pair", scatter_dimension=0, tiled=True)


def kernel(dims, fac, amp, out, own, nb, fact, tall, tt, wst, red, part, recv, send, fsend, frecv, lsem, xs, xr):
    nx, nz, ny, nk = dims
    nv = nz * ny * nk
    blocks, aux, virt = fac.shape
    pairs, rows, _ = amp.shape
    group = 2 * rows
    groups = virt // group
    wide = 2 * pairs * rows

    x = lax.axis_index("pair")
    v = lax.axis_index("vblk")
    z, y, k = v // (ny * nk), (v // nk) % ny, v % nk

    def place(zz, yy, kk):
        return (zz * ny + yy) * nk + kk

    zs = [lax.rem(z + i, nz) for i in range(nz)]
    nxt, prv = lax.rem(v + 1, nv), lax.rem(v + nv - 1, nv)
    to_y, to_k = (x, place(z, 1 - y, k)), (x, place(z, y, 1 - k))
    to_x = (1 - x, v)

    barrier = pltpu.get_barrier_semaphore()
    peers = [(x, place(zz, y, k)) for zz in zs[1:]] + [to_y, to_k, to_x, (x, nxt), (x, prv)]
    for peer in peers:
        pl.semaphore_signal(barrier, inc=1, device_id=peer, device_id_type=MESH)
    pl.semaphore_wait(barrier, len(peers))

    sends = []

    def push(src, piece, target):
        copy = pltpu.make_async_remote_copy(
            src_ref=src,
            dst_ref=tall.at[piece],
            send_sem=send.at[len(sends)],
            recv_sem=recv.at[piece],
            device_id=target,
            device_id_type=MESH,
        )
        copy.start()
        sends.append(copy)

    def arrived(piece):
        pltpu.make_async_remote_copy(
            src_ref=amp,
            dst_ref=tall.at[piece],
            send_sem=send.at[0],
            recv_sem=recv.at[piece],
            device_id=to_x,
            device_id_type=MESH,
        ).wait_recv()

    def factor(j):
        return pltpu.make_async_remote_copy(
            src_ref=fac.at[j],
            dst_ref=nb.at[j],
            send_sem=fsend.at[j],
            recv_sem=frecv.at[j],
            device_id=(x, nxt),
            device_id_type=MESH,
        )

    def load(j):
        return pltpu.make_async_copy(fac.at[j], own.at[j], lsem.at[j])

    mine = x * nv + v
    for zz in zs[1:]:
        push(amp, mine, (x, place(zz, y, k)))
    push(amp, mine, to_y)
    push(amp, mine, to_x)
    push(amp, mine, to_k)
    factor(0).start()
    for j in range(blocks):
        load(j).start()
    tall[pl.ds(mine, 1)] = amp[...][None]

    def stage_z():
        for zz in zs[1:]:
            piece = x * nv + place(zz, y, k)
            arrived(piece)
            for target in (to_y, to_x, to_k):
                push(tall.at[piece], piece, target)

    def stage_y():
        for zz in zs:
            piece = x * nv + place(zz, 1 - y, k)
            arrived(piece)
            for target in (to_x, to_k):
                push(tall.at[piece], piece, target)

    def stage_x(ys):
        for yy in ys:
            for zz in zs:
                piece = (1 - x) * nv + place(zz, yy, k)
                arrived(piece)
                push(tall.at[piece], piece, to_k)

    def stage_k():
        for xx in (x, 1 - x):
            for yy in (y, 1 - y):
                for zz in zs:
                    arrived(xx * nv + place(zz, yy, 1 - k))

    def integrals(src, j, slot):
        def one(a, _):
            w = jnp.dot(fact[a], src[j], preferred_element_type=F32)
            high = w.astype(BF16)
            wst[slot, 0, a] = high
            wst[slot, 1, a] = (w - high.astype(F32)).astype(BF16)
            return 0

        lax.fori_loop(0, blocks, one, 0)

    def contract(slot, panel):
        lhs = jnp.concatenate(
            [
                wst[slot, :, :, g * group : (g + 1) * group, :].reshape(2 * blocks * group, virt)
                for g in range(groups)
            ],
            axis=1,
        )
        rhs = tt[...].reshape(groups * virt, wide)
        full = jnp.dot(lhs, rhs, preferred_element_type=F32).reshape(2, blocks, group, wide)
        full = full[0] + full[1]
        row = lax.broadcasted_iota(jnp.int32, (blocks, group, wide), 1)
        col = lax.broadcasted_iota(jnp.int32, (blocks, group, wide), 2)
        diag = (col // (pairs * rows)) * rows + col % rows
        red[panel] = jnp.sum(jnp.where(row == diag, full, 0.0), axis=1)

    def contract_own(j, _):
        contract(j, j)
        return 0

    def turn_amp(g, _):
        tt[g] = tall[pl.ds(2 * g, 2)].reshape(wide, virt).T
        return 0

    def turn(a, _):
        fact[a] = own[a].T
        return 0

    for j in range(blocks):
        load(j).wait()
    lax.fori_loop(0, blocks, turn, 0)
    integrals(own, 0, 0)
    integrals(own, 1, 1)
    stage_z()
    for j in range(1, blocks):
        factor(j).start()
    for j in range(2, blocks):
        integrals(own, j, j)
    stage_y()
    factor(0).wait_recv()
    integrals(nb, 0, blocks)
    stage_x([y])
    stage_x([1 - y])
    stage_k()
    lax.fori_loop(0, groups, turn_amp, 0)
    lax.fori_loop(0, blocks, contract_own, 0)
    contract(blocks, blocks)
    for j in range(1, blocks):
        factor(j).wait_recv()
        integrals(nb, j, j - 1)
        contract(j - 1, blocks + j)

    swap = pltpu.make_async_remote_copy(
        src_ref=red, dst_ref=part, send_sem=xs, recv_sem=xr, device_id=to_x, device_id_type=MESH
    )
    swap.start()
    for copy in sends:
        copy.wait_send()
    for j in range(blocks):
        factor(j).wait_send()
    swap.wait()
    out[...] = red[...] + part[...]


def staged_body(dims, factors, amplitudes):
    aux, blocks, virt = factors.shape
    pairs, rows, _ = amplitudes.shape
    pieces = dims[0] * dims[1] * dims[2] * dims[3]
    wide = 2 * pairs * rows
    nsends = 3 * (dims[1] - 1) + (dims[1] + 2) + 2 * dims[1] + 2 * dims[1]
    vmem = pl.BlockSpec(memory_space=pltpu.VMEM)
    sums = pl.pallas_call(
        functools.partial(kernel, dims),
        out_shape=jax.ShapeDtypeStruct((STEPS * blocks, blocks, wide), F32),
        in_specs=[pl.BlockSpec(memory_space=pl.ANY), vmem],
        out_specs=vmem,
        scratch_shapes=[
            pltpu.VMEM((blocks, aux, virt), BF16),
            pltpu.VMEM((blocks, aux, virt), BF16),
            pltpu.VMEM((blocks, virt, aux), BF16),
            pltpu.VMEM((pieces, pairs, rows, virt), BF16),
            pltpu.VMEM((virt // (2 * rows), virt, wide), BF16),
            pltpu.VMEM((blocks + 1, 2, blocks, virt, virt), BF16),
            pltpu.VMEM((STEPS * blocks, blocks, wide), F32),
            pltpu.VMEM((STEPS * blocks, blocks, wide), F32),
            pltpu.SemaphoreType.DMA((pieces,)),
            pltpu.SemaphoreType.DMA((pieces,)),
            pltpu.SemaphoreType.DMA((blocks,)),
            pltpu.SemaphoreType.DMA((blocks,)),
            pltpu.SemaphoreType.DMA((blocks,)),
            pltpu.SemaphoreType.DMA,
            pltpu.SemaphoreType.DMA,
        ],
        compiler_params=pltpu.CompilerParams(
            collective_id=0, has_side_effects=True, vmem_limit_bytes=60 * 1024 * 1024
        ),
    )(factors.transpose(1, 0, 2), amplitudes)
    share = pairs // dims[0]
    sums = sums.reshape(STEPS, blocks, blocks, 2, pairs, rows).sum(axis=(3, 5))
    sums = sums.transpose(3, 2, 0, 1)
    return lax.dynamic_slice_in_dim(sums, lax.axis_index("pair") * share, share, 0)


def solution(mesh):
    placed = (P("pair", "vblk", None), P(None, ("pair", "vblk"), None))
    staged = mesh.shape["pair"] == 2 and mesh.shape["vblk"] == 16
    body = functools.partial(staged_body, (2, 4, 2, 2)) if staged else general_body
    return jax.shard_map(
        body, mesh=mesh, in_specs=placed, out_specs=P("pair", "vblk", None, None), check_vma=False
    )
```

```python
import functools
import math

import jax
import jax.numpy as jnp
from jax import lax
from jax.experimental import pallas as pl
from jax.experimental.pallas import tpu as pltpu
from jax.sharding import PartitionSpec as P

STEPS = 2
MESH = pl.DeviceIdType.MESH
F32 = jnp.float32
BF16 = jnp.bfloat16


def shifted(value, axis, steps):
    count = lax.axis_size(axis)
    pairs = [(source, (source + steps) % count) for source in range(count)]
    return lax.ppermute(value, axis, pairs)


def general_body(factors, amplitudes):
    aux_rows = factors.shape[0]
    block_rows = factors.shape[1]
    pair_count = amplitudes.shape[0]
    virtuals = amplitudes.shape[2]
    partner = jnp.concatenate([factors, shifted(factors, "vblk", 1)], axis=1)
    running = jnp.zeros((pair_count, block_rows, STEPS * block_rows), F32)
    amp_piece = lax.all_gather(amplitudes, ("pair", "vblk"), axis=1, tiled=True)
    row_count = amp_piece.shape[1]
    group_size = math.gcd(row_count, 64)
    block_count = row_count // group_size
    piece_blocks = amp_piece.reshape(pair_count, block_count, group_size, virtuals).transpose(
        1, 0, 2, 3
    )
    own_parts = factors.reshape(aux_rows, block_rows, block_count, group_size).transpose(2, 0, 1, 3)

    def one_block(carried, pieces):
        piece_part, own_part = pieces
        integrals = jnp.einsum("qac,qbd->acbd", own_part, partner, preferred_element_type=F32)
        update = jnp.einsum(
            "pcd,acbd->pab", piece_part.astype(F32), integrals, precision=lax.Precision.HIGHEST
        )
        return (carried + update, None)

    running, unused = lax.scan(one_block, running, (piece_blocks, own_parts))
    partial_ladder = running.reshape(pair_count, block_rows, STEPS, block_rows)
    return lax.psum_scatter(partial_ladder, "pair", scatter_dimension=0, tiled=True)


def kernel(dims, fac, amp, out, own, nb, fact, tall, tt, wst, red, part, recv, send, fsend, frecv, lsem, xs, xr):
    nx, nz, ny, nk = dims
    nv = nz * ny * nk
    blocks, aux, virt = fac.shape
    pairs, rows, _ = amp.shape
    group = 2 * rows
    groups = virt // group
    wide = 2 * pairs * rows

    x = lax.axis_index("pair")
    v = lax.axis_index("vblk")
    z, y, k = v // (ny * nk), (v // nk) % ny, v % nk

    def place(zz, yy, kk):
        return (zz * ny + yy) * nk + kk

    zs = [lax.rem(z + i, nz) for i in range(nz)]
    nxt, prv = lax.rem(v + 1, nv), lax.rem(v + nv - 1, nv)
    to_y, to_k = (x, place(z, 1 - y, k)), (x, place(z, y, 1 - k))
    to_x = (1 - x, v)

    barrier = pltpu.get_barrier_semaphore()
    peers = [(x, place(zz, y, k)) for zz in zs[1:]] + [to_y, to_k, to_x, (x, nxt), (x, prv)]
    for peer in peers:
        pl.semaphore_signal(barrier, inc=1, device_id=peer, device_id_type=MESH)
    pl.semaphore_wait(barrier, len(peers))

    sends = []

    def push(src, piece, target):
        copy = pltpu.make_async_remote_copy(
            src_ref=src,
            dst_ref=tall.at[piece],
            send_sem=send.at[len(sends)],
            recv_sem=recv.at[piece],
            device_id=target,
            device_id_type=MESH,
        )
        copy.start()
        sends.append(copy)

    def arrived(piece):
        pltpu.make_async_remote_copy(
            src_ref=amp,
            dst_ref=tall.at[piece],
            send_sem=send.at[0],
            recv_sem=recv.at[piece],
            device_id=to_x,
            device_id_type=MESH,
        ).wait_recv()

    def factor(j):
        return pltpu.make_async_remote_copy(
            src_ref=fac.at[j],
            dst_ref=nb.at[j],
            send_sem=fsend.at[j],
            recv_sem=frecv.at[j],
            device_id=(x, nxt),
            device_id_type=MESH,
        )

    def load(j):
        return pltpu.make_async_copy(fac.at[j], own.at[j], lsem.at[j])

    mine = x * nv + v
    for zz in zs[1:]:
        push(amp, mine, (x, place(zz, y, k)))
    push(amp, mine, to_y)
    push(amp, mine, to_x)
    push(amp, mine, to_k)
    factor(0).start()
    for j in range(blocks):
        load(j).start()
    tall[pl.ds(mine, 1)] = amp[...][None]

    def stage_z():
        for zz in zs[1:]:
            piece = x * nv + place(zz, y, k)
            arrived(piece)
            for target in (to_y, to_x, to_k):
                push(tall.at[piece], piece, target)

    def stage_y():
        for zz in zs:
            piece = x * nv + place(zz, 1 - y, k)
            arrived(piece)
            for target in (to_x, to_k):
                push(tall.at[piece], piece, target)

    def stage_x(ys):
        for yy in ys:
            for zz in zs:
                piece = (1 - x) * nv + place(zz, yy, k)
                arrived(piece)
                push(tall.at[piece], piece, to_k)

    def stage_k():
        for xx in (x, 1 - x):
            for yy in (y, 1 - y):
                for zz in zs:
                    arrived(xx * nv + place(zz, yy, 1 - k))

    def integrals(src, j, slot):
        def one(a, _):
            w = jnp.dot(fact[a], src[j], preferred_element_type=F32)
            high = w.astype(BF16)
            wst[slot, 0, a] = high
            wst[slot, 1, a] = (w - high.astype(F32)).astype(BF16)
            return 0

        lax.fori_loop(0, blocks, one, 0)

    def contract(slot, panel):
        lhs = jnp.concatenate(
            [
                wst[slot, :, :, g * group : (g + 1) * group, :].reshape(2 * blocks * group, virt)
                for g in range(groups)
            ],
            axis=1,
        )
        rhs = tt[...].reshape(groups * virt, wide)
        full = jnp.dot(lhs, rhs, preferred_element_type=F32).reshape(2, blocks, group, wide)
        full = full[0] + full[1]
        row = lax.broadcasted_iota(jnp.int32, (blocks, group, wide), 1)
        col = lax.broadcasted_iota(jnp.int32, (blocks, group, wide), 2)
        diag = (col // (pairs * rows)) * rows + col % rows
        red[panel] = jnp.sum(jnp.where(row == diag, full, 0.0), axis=1)

    def contract_own(j, _):
        contract(j, j)
        return 0

    def turn_amp(g, _):
        tt[g] = tall[pl.ds(2 * g, 2)].reshape(wide, virt).T
        return 0

    def turn(a, _):
        fact[a] = own[a].T
        return 0

    for j in range(blocks):
        load(j).wait()
    lax.fori_loop(0, blocks, turn, 0)
    integrals(own, 0, 0)
    integrals(own, 1, 1)
    stage_z()
    for j in range(2, blocks):
        integrals(own, j, j)
    stage_y()
    factor(0).wait_recv()
    integrals(nb, 0, blocks)
    stage_x([y])
    stage_x([1 - y])
    for j in range(1, blocks):
        factor(j).start()
    stage_k()
    lax.fori_loop(0, groups, turn_amp, 0)
    lax.fori_loop(0, blocks, contract_own, 0)
    contract(blocks, blocks)
    for j in range(1, blocks):
        factor(j).wait_recv()
        integrals(nb, j, j - 1)
        contract(j - 1, blocks + j)

    swap = pltpu.make_async_remote_copy(
        src_ref=red, dst_ref=part, send_sem=xs, recv_sem=xr, device_id=to_x, device_id_type=MESH
    )
    swap.start()
    for copy in sends:
        copy.wait_send()
    for j in range(blocks):
        factor(j).wait_send()
    swap.wait()
    out[...] = red[...] + part[...]


def staged_body(dims, factors, amplitudes):
    aux, blocks, virt = factors.shape
    pairs, rows, _ = amplitudes.shape
    pieces = dims[0] * dims[1] * dims[2] * dims[3]
    wide = 2 * pairs * rows
    nsends = 3 * (dims[1] - 1) + (dims[1] + 2) + 2 * dims[1] + 2 * dims[1]
    vmem = pl.BlockSpec(memory_space=pltpu.VMEM)
    sums = pl.pallas_call(
        functools.partial(kernel, dims),
        out_shape=jax.ShapeDtypeStruct((STEPS * blocks, blocks, wide), F32),
        in_specs=[pl.BlockSpec(memory_space=pl.ANY), vmem],
        out_specs=vmem,
        scratch_shapes=[
            pltpu.VMEM((blocks, aux, virt), BF16),
            pltpu.VMEM((blocks, aux, virt), BF16),
            pltpu.VMEM((blocks, virt, aux), BF16),
            pltpu.VMEM((pieces, pairs, rows, virt), BF16),
            pltpu.VMEM((virt // (2 * rows), virt, wide), BF16),
            pltpu.VMEM((blocks + 1, 2, blocks, virt, virt), BF16),
            pltpu.VMEM((STEPS * blocks, blocks, wide), F32),
            pltpu.VMEM((STEPS * blocks, blocks, wide), F32),
            pltpu.SemaphoreType.DMA((pieces,)),
            pltpu.SemaphoreType.DMA((pieces,)),
            pltpu.SemaphoreType.DMA((blocks,)),
            pltpu.SemaphoreType.DMA((blocks,)),
            pltpu.SemaphoreType.DMA((blocks,)),
            pltpu.SemaphoreType.DMA,
            pltpu.SemaphoreType.DMA,
        ],
        compiler_params=pltpu.CompilerParams(
            collective_id=0, has_side_effects=True, vmem_limit_bytes=60 * 1024 * 1024
        ),
    )(factors.transpose(1, 0, 2), amplitudes)
    share = pairs // dims[0]
    sums = sums.reshape(STEPS, blocks, blocks, 2, pairs, rows).sum(axis=(3, 5))
    sums = sums.transpose(3, 2, 0, 1)
    return lax.dynamic_slice_in_dim(sums, lax.axis_index("pair") * share, share, 0)


def solution(mesh):
    placed = (P("pair", "vblk", None), P(None, ("pair", "vblk"), None))
    staged = mesh.shape["pair"] == 2 and mesh.shape["vblk"] == 16
    body = functools.partial(staged_body, (2, 4, 2, 2)) if staged else general_body
    return jax.shard_map(
        body, mesh=mesh, in_specs=placed, out_specs=P("pair", "vblk", None, None), check_vma=False
    )
```
